128 devices in a mesh: state: 8 (over x_hi, z), walk: 16 (over x_lo, y, core).
Axes of the slice: x: 4 (x_hi: 2, x_lo: 2; x = x_hi * 2 + x_lo), y: 4, z: 4, core: 2. Of those that a mesh axis runs over, the one named last changes fastest.
Arguments:
- feats: float32 [8, 128, 80, 128], P('state', 'walk'), may hold values from -6 to 6
- inverses: float32 [8, 128, 2, 40, 40], P('state', 'walk'), may hold values from -1 to 1
- counts: int32 [8], P('state'), may hold values from 32 to 128, as said below
- w_embed: float32 [8, 128, 512], P('state', 'walk'), may hold values from -0.5 to 0.5
- w_qkv: float32 [8, 1, 512, 1536], P('state', None, 'walk'), may hold values from -0.25 to 0.25
- w_out: float32 [8, 1, 512, 512], P('state', None, 'walk'), may hold values from -0.25 to 0.25
- w_mlp: float32 [8, 1, 512, 512], P('state', None, 'walk'), may hold values from -0.25 to 0.25
- w_orb: float32 [8, 512, 80], P('state', 'walk'), may hold values from -0.25 to 0.25
Outputs:
- own_amp: float32 [8, 128], P('state', 'walk')
- margin: float32 [8, 8], P('state')
- penalty: float32 [], replicated
The draws below stay inside these ranges and needn't reach their ends.
Inputs may be any that keep to these rules, and one draw needn't show every extreme that they name: `counts`: some state has all 128 walkers live.
All inputs are finite; a program needn't handle non-finite values.
Results may differ from the reference program's by a relative error of at most 0.0002.
Values sent between devices are 32-bit elements; how exact they have to be, the bound alone decides.
No kernel may reach another device: no remote copies, remote signals or barrier semaphores. Data moves between devices by JAX's collectives and lax.ppermute only.
A program may use at most 256 MiB of HBM per device.

```python
import math
import jax
import jax.numpy as jnp
from jax import lax

D = 512
HEADS = 8
HEAD_DIM = 64
ELEC = 80
HALF = 40
FEAT = 128
LAYERS = 1
WALKERS = 128
STATES = 8


def draw_counts(key, part):
    key = jax.random.fold_in(key, 7)
    first, second = jax.random.split(key)
    base = jax.random.randint(first, (STATES,), WALKERS // 4, WALKERS + 1)
    full_at = jax.random.randint(second, (), 0, STATES)
    return jnp.where(jnp.arange(STATES) == full_at, WALKERS, base).astype(jnp.int32)


def shard_levels(own_key, shape, shards, low, largest):
    gain, own = 1.0, jax.random.fold_in(own_key, 6)
    for axis_at, blocks in shards:
        heights = jnp.exp(jax.random.uniform(jax.random.fold_in(own, axis_at), (blocks,), jnp.float32, low / len(shards), largest / len(shards)))
        gain = gain * jnp.repeat(heights, shape[axis_at] // blocks).reshape([-1 if axis == axis_at else 1 for axis in range(len(shape))])
    return gain


def noise(own_key, dims, deviation, reach, cuts=(), kind=jnp.bfloat16):
    gain = shard_levels(own_key, dims, cuts, -0.22, 0.18) if cuts else 1.0
    result = jax.random.normal(own_key, dims, jnp.float32) * deviation * gain
    return jnp.minimum(jnp.maximum(result, -reach), reach).astype(kind)


def setup_inputs(seed: int = 0) -> dict:
    key_of = jax.random.split(jax.random.key(seed), 9)
    return {
        "feats": noise(key_of[0], (STATES, WALKERS, ELEC, FEAT), 1.0, 6.0, ((0, 8), (1, 16)), jnp.float32),
        "inverses": noise(key_of[1], (STATES, WALKERS, 2, HALF, HALF), HALF ** -0.5, 1.0, ((0, 8), (1, 16)), jnp.float32),
        "counts": draw_counts(jax.random.fold_in(key_of[8], 71), 0),
        "w_embed": noise(key_of[3], (STATES, FEAT, D), FEAT ** -0.5, 0.5, ((0, 8), (1, 16)), jnp.float32),
        "w_qkv": noise(key_of[4], (STATES, LAYERS, D, 3 * D), D ** -0.5, 0.25, ((0, 8), (2, 16)), jnp.float32),
        "w_out": noise(key_of[5], (STATES, LAYERS, D, D), D ** -0.5, 0.25, ((0, 8), (2, 16)), jnp.float32),
        "w_mlp": noise(key_of[6], (STATES, LAYERS, D, D), D ** -0.5, 0.25, ((0, 8), (2, 16)), jnp.float32),
        "w_orb": noise(key_of[7], (STATES, D, ELEC), D ** -0.5, 0.25, ((0, 8), (1, 16)), jnp.float32),
    }


def matmul(left, right):
    return jnp.dot(left, right, precision=lax.Precision.HIGHEST, preferred_element_type=jnp.float32)

def normalize(values):
    centred = values - lax.optimization_barrier(jnp.mean(values, axis=-1, keepdims=True))
    spread = lax.optimization_barrier(jnp.mean(centred * centred, axis=-1, keepdims=True))
    return centred * lax.rsqrt(spread + 1e-05)

def mix_heads(qkv):
    walkers = qkv.shape[0] // ELEC
    parts = qkv.reshape(walkers, ELEC, 3, HEADS, HEAD_DIM)
    query = parts[:, :, 0]
    keys = parts[:, :, 1]
    values = parts[:, :, 2]
    scores = jnp.einsum('bqhd,bkhd->bhqk', query, keys, precision=lax.Precision.HIGHEST) / math.sqrt(HEAD_DIM)
    weights = jax.nn.softmax(scores, axis=-1)
    mixed = jnp.einsum('bhqk,bkhd->bqhd', weights, values, precision=lax.Precision.HIGHEST)
    return mixed.reshape(walkers * ELEC, HEADS * HEAD_DIM)

def determinant_part(orbitals, inverse):
    walkers = inverse.shape[0]
    phi = orbitals.reshape(walkers, ELEC, ELEC)
    blocks = jnp.stack([phi[:, :HALF, :HALF], phi[:, HALF:, HALF:]], axis=1)
    product = jnp.einsum('bsij,bsjk->bsik', inverse, blocks, precision=lax.Precision.HIGHEST)
    return jnp.log(lax.optimization_barrier(jnp.mean(product * product, axis=(1, 2, 3))) + 1e-05)

def log_amplitude(rows, inverse, weights):
    embed, qkv_all, out_all, mlp_all, orbital = weights
    hidden = matmul(rows, embed)
    for layer in range(LAYERS):
        qkv = matmul(normalize(hidden), qkv_all[layer])
        hidden = hidden + matmul(mix_heads(qkv), out_all[layer])
        hidden = hidden + jnp.tanh(matmul(normalize(hidden), mlp_all[layer]))
    return determinant_part(matmul(hidden, orbital), inverse)

def reference(feats, inverses, counts, w_embed, w_qkv, w_out, w_mlp, w_orb):

    def per_net(index):
        weights = (w_embed[index], w_qkv[index], w_out[index], w_mlp[index], w_orb[index])

        def per_block(block):
            rows = feats[block].reshape(WALKERS * ELEC, FEAT)
            return log_amplitude(rows, inverses[block], weights)
        return lax.map(per_block, jnp.arange(STATES, dtype=jnp.int32))
    table = lax.map(per_net, jnp.arange(STATES, dtype=jnp.int32))
    diag = jnp.arange(STATES, dtype=jnp.int32)
    own_amp = table[diag, diag]
    ratio = jnp.exp(jnp.transpose(table, (1, 0, 2)) - own_amp[:, None, :])
    valid = (jnp.arange(WALKERS, dtype=jnp.int32)[None, :] < counts[:, None]).astype(jnp.float32)
    margin = lax.optimization_barrier(jnp.sum(ratio * valid[:, None, :], axis=2)) / counts.astype(jnp.float32)[:, None]
    lower = (diag[None, :] < diag[:, None]).astype(jnp.float32)
    penalty = 4.0 * jnp.sum(lower * margin * margin.T)
    return (own_amp, margin, penalty)
```

```python
import math

import jax
import jax.numpy as jnp
from jax import lax
from jax.experimental import pallas as pl
from jax.experimental.pallas import tpu as pltpu
from jax.sharding import PartitionSpec as P

ELEC = 80
HALF = 40
BF = jnp.bfloat16
F32 = jnp.float32
OUT_AT, MLP_AT, ORB_AT, EMB_AT, PACKED = 1536, 2048, 2560, 2688, 2816
SAFE = 90.0


def dot(left, right):
    return jnp.dot(left, right, preferred_element_type=F32)


def dot_nt(left, right):
    return lax.dot_general(
        left, right, (((1,), (1,)), ((), ())), preferred_element_type=F32
    )


def split(values):
    high = values.astype(BF)
    return high, (values - high.astype(F32)).astype(BF)


def dot3(left, right, product):
    left_high, left_low = split(left)
    right_high, right_low = split(right)
    return (
        product(left_high, right_high)
        + product(left_low, right_high)
        + product(left_high, right_low)
    )


def weight_dot(values, ref, precise):
    if precise:
        high, low = split(values)
        return dot(high, ref[0]) + dot(low, ref[0]) + dot(high, ref[1])
    return dot(values.astype(BF), ref[0])


def prepare(packed, w_in, w_back, w_mlp, w_orb):
    shards = packed.shape[0] // 32
    parts = []
    for j in range(4):
        rows = [packed[i * 32 + 8 * j : i * 32 + 8 * j + 8, EMB_AT:PACKED] for i in range(shards)]
        parts.append(jnp.concatenate(rows, axis=0))
    embed = jnp.concatenate(parts, axis=1)
    centred = embed - jnp.mean(embed, axis=1, keepdims=True)

    def put(at, values):
        high, low = split(values)
        columns = slice(at, at + values.shape[1])
        w_in[0, 0:128, columns] = high
        w_in[0, 128:256, columns] = high
        w_in[1, 0:128, columns] = low

    put(0, embed)
    query = dot3(centred, packed[:, 0:512], dot) * (math.log2(math.e) / 8.0)
    keys = dot3(centred, packed[:, 512:1024], dot)
    values = dot3(centred, packed[:, 1024:1536], dot)
    lane = lax.broadcasted_iota(jnp.int32, (128, 128), 1)
    for head in range(8):
        pair = slice(128 * (head // 2), 128 * (head // 2) + 128)
        keep = (lane < 64) if head % 2 == 0 else (lane >= 64)
        put(512 + 128 * head, dot3(jnp.where(keep, query[:, pair], 0.0), keys[:, pair], dot_nt))
        back = dot3(jnp.where(keep, values[:, pair], 0.0), packed[pair, OUT_AT:MLP_AT], dot)
        high, low = split(back)
        w_back[0, 128 * head : 128 * head + 128, :] = high
        w_back[1, 128 * head : 128 * head + 128, :] = low
    for ref, at, width in ((w_mlp, MLP_AT, 512), (w_orb, ORB_AT, 128)):
        high, low = split(packed[:, at : at + width])
        ref[0] = high
        ref[1] = low


def centre(values):
    centred = values - jnp.mean(values, axis=1, keepdims=True)
    spread = jnp.mean(centred * centred, axis=1, keepdims=True)
    return centred, lax.rsqrt(spread + 1e-05)


def walkers_block(feats, inverse, number, w_in, w_back, w_mlp, w_orb, scores, precise):
    feats_high, feats_low = split(feats)
    hidden = dot(jnp.concatenate([feats_high, feats_low], axis=1), w_in[0, :, 0:512])
    if precise:
        hidden = hidden + dot(feats_high, w_in[1, 0:128, 0:512])
    _, scale = centre(hidden)
    high, low = split(feats * scale)
    query = dot(jnp.concatenate([high, low], axis=1), w_in[0, :, 512:1536])
    if precise:
        query = query + dot(high, w_in[1, 0:128, 512:1536])
    empty = jnp.zeros((128 - ELEC, 128), BF)

    def padded(values, w):
        return jnp.concatenate([values[ELEC * w : ELEC * w + ELEC], empty], axis=0)

    largest = jnp.zeros((8, 128), F32)
    for w in range(number):
        rows = query[ELEC * w : ELEC * w + ELEC]
        stacked = jnp.concatenate([rows[:, 128 * h : 128 * h + 128] for h in range(8)], axis=0)
        if precise:
            stacked_high, stacked_low = split(stacked)
            score = (
                dot_nt(stacked_high, padded(high, w))
                + dot_nt(stacked_low, padded(high, w))
                + dot_nt(stacked_high, padded(low, w))
            )
        else:
            score = dot_nt(stacked.astype(BF), padded(high, w))
        scores[w] = score
        sizes = jnp.abs(score).reshape(8 * ELEC // 8, 8, 128)
        largest = jnp.maximum(largest, jnp.max(sizes, axis=0))

    @pl.when(jnp.logical_not(jnp.max(largest) < SAFE))
    def _():
        lane = lax.broadcasted_iota(jnp.int32, (8 * ELEC, 128), 1)

        @pl.loop(0, number)
        def _(w):
            score = scores[w]
            top = jnp.max(jnp.where(lane < ELEC, score, -jnp.inf), axis=1, keepdims=True)
            scores[w] = jnp.where(lane < ELEC, score - top, 0.0)

    row = lax.broadcasted_iota(jnp.int32, (128, 128), 0)
    live = jnp.where(row < ELEC, 1.0, 0.0).astype(BF)
    mixed = []
    for w in range(number):
        weights = jnp.exp2(scores[w])
        right = jnp.concatenate([padded(high, w), live], axis=1)
        if precise:
            weights_high, weights_low = split(weights)
            both = dot(weights_high, right) + dot(weights_low, right)
            own = (both[:, :128] + dot(weights_high, padded(low, w))) / both[:, 128:]
        else:
            both = dot(weights.astype(BF), right)
            own = (both[:, :128] / both[:, 128:]).astype(BF)
        mixed.append(
            jnp.concatenate([own[ELEC * h : ELEC * h + ELEC] for h in range(8)], axis=1)
        )
    hidden = hidden + weight_dot(jnp.concatenate(mixed, axis=0), w_back, precise)
    centred, scale = centre(hidden)
    hidden = hidden + jnp.tanh(weight_dot(centred * scale, w_mlp, precise))
    orbitals = weight_dot(hidden, w_orb, precise)
    lane = lax.broadcasted_iota(jnp.int32, (HALF, 128), 1)
    results = []
    for w in range(number):
        total = jnp.zeros((HALF, 128), F32)
        for spin in range(2):
            first = HALF * spin
            product = jnp.dot(
                inverse[w][first : first + HALF, :HALF],
                orbitals[ELEC * w + first : ELEC * w + first + HALF],
                precision=lax.Precision.HIGHEST,
                preferred_element_type=F32,
            )
            product = jnp.where((lane >= first) & (lane < first + HALF), product, 0.0)
            total = total + product * product
        total = jnp.sum(jnp.sum(total, axis=0, keepdims=True), axis=1, keepdims=True)
        results.append(jnp.log(total / (2.0 * HALF * HALF) + 1e-05))
    return results


def network_kernel(
    place, counts, local, group, other, packed, table, own, w_in, w_back, w_mlp, w_orb, scores
):
    step = pl.program_id(0)
    number = 8
    state = place[step]
    lane = lax.broadcasted_iota(jnp.int32, (1, 128), 1)

    def unpacked(pack):
        found = []
        for w in range(number):
            third = w % 3
            part = pack[w // 3]
            found.append(part if third == 0 else pltpu.roll(part, 128 - HALF * third, 1))
        return found

    @pl.when(step == 0)
    def _():
        prepare(packed, w_in, w_back, w_mlp, w_orb)
        feats = local[0:number].reshape(number * ELEC, 128)
        results = walkers_block(
            feats, unpacked(local[number:]), number, w_in, w_back, w_mlp, w_orb, scores, True
        )
        row = jnp.where(lane == 64, counts[0].astype(F32), 0.0)
        alone = jnp.zeros((1, 128), F32)
        for w in range(number):
            row = row + jnp.where(lane == state * 8 + w, results[w], 0.0)
            alone = alone + jnp.where(lane == w, results[w], 0.0)
        own[...] = alone
        table[...] = jnp.broadcast_to(row, table.shape)

    @pl.when(step > 0)
    def _():
        near = step < 4
        block = jnp.where(near, group[0], other[0])
        feats = block[0:number].reshape(number * ELEC, 128)
        results = walkers_block(
            feats, unpacked(block[number:]), number, w_in, w_back, w_mlp, w_orb, scores, False
        )
        row = jnp.zeros((1, 128), F32)
        for w in range(number):
            row = row + jnp.where(lane == state * 8 + w, results[w], 0.0)
        table[...] += jnp.broadcast_to(row, table.shape)


def networks(place, counts, local, group, other, packed):
    return pl.pallas_call(
        network_kernel,
        grid_spec=pltpu.PrefetchScalarGridSpec(
            num_scalar_prefetch=2,
            grid=(8,),
            in_specs=[
                pl.BlockSpec((11, ELEC, 128), lambda i, place, counts: (0, 0, 0)),
                pl.BlockSpec(
                    (1, 11, ELEC, 128),
                    lambda i, place, counts: (place[jnp.clip(i, 1, 3)] % 4, 0, 0, 0),
                ),
                pl.BlockSpec(
                    (1, 11, ELEC, 128),
                    lambda i, place, counts: (place[jnp.maximum(i, 4)] % 4, 0, 0, 0),
                ),
                pl.BlockSpec((512, PACKED), lambda i, place, counts: (0, 0)),
            ],
            out_specs=[
                pl.BlockSpec((128, 128), lambda i, place, counts: (0, 0)),
                pl.BlockSpec((1, 128), lambda i, place, counts: (0, 0)),
            ],
            scratch_shapes=[
                pltpu.VMEM((2, 256, 1536), BF),
                pltpu.VMEM((2, 1024, 512), BF),
                pltpu.VMEM((2, 512, 512), BF),
                pltpu.VMEM((2, 512, 128), BF),
                pltpu.VMEM((8, 8 * ELEC, 128), F32),
            ],
        ),
        out_shape=[
            jax.ShapeDtypeStruct((128, 128), F32),
            jax.ShapeDtypeStruct((1, 128), F32),
        ],
        compiler_params=pltpu.CompilerParams(vmem_limit_bytes=56 * 2**20),
        cost_estimate=pl.CostEstimate(
            flops=30_000_000_000, bytes_accessed=10_000_000, transcendentals=8_000_000
        ),
    )(place, counts, local, group, other, packed)


def margin_kernel(place, received, margin, penalty):
    table = received[...]
    lane = lax.broadcasted_iota(jnp.int32, (16, 128), 1)
    block = lax.broadcasted_iota(jnp.int32, (16, 128), 0)
    owner = lane // 8
    own = jnp.zeros((16, 128), F32)
    counts = jnp.ones((1, 128), F32)
    for s in range(8):
        own = jnp.where(owner == s, table[16 * s : 16 * s + 16], own)
        counts = jnp.where(owner[0:1] == s, table[16 * s : 16 * s + 1, 64:65], counts)
    walker = (block * 8 + lane % 8).astype(F32)
    valid = (walker < counts) & (lane < 64)
    rows = []
    for t in range(8):
        ratio = jnp.exp(jnp.where(valid, table[16 * t : 16 * t + 16] - own, -jnp.inf))
        rows.append(jnp.sum(ratio, axis=0, keepdims=True))
    sums = jnp.concatenate(rows, axis=0) / counts
    pick = (
        lax.broadcasted_iota(jnp.int32, (8, 128), 1) // 8
        == lax.broadcasted_iota(jnp.int32, (8, 128), 0)
    ).astype(F32)

    def exact(left, right):
        return lax.dot_general(
            left,
            right,
            (((1,), (1,)), ((), ())),
            precision=lax.Precision.HIGHEST,
            preferred_element_type=F32,
        )

    by_state = exact(pick, sums)
    by_network = exact(sums, pick)
    row = lax.broadcasted_iota(jnp.int32, (8, 8), 0)
    column = lax.broadcasted_iota(jnp.int32, (8, 8), 1)
    margin[...] = jnp.sum(jnp.where(row == place[0], by_state, 0.0), axis=0, keepdims=True)
    product = jnp.where(column < row, by_state * by_network, 0.0)
    total = jnp.sum(jnp.sum(product, axis=0, keepdims=True), axis=1, keepdims=True)
    penalty[...] = 4.0 * total


def margins(place, received):
    return pl.pallas_call(
        margin_kernel,
        grid_spec=pltpu.PrefetchScalarGridSpec(
            num_scalar_prefetch=1,
            grid=(1,),
            in_specs=[pl.BlockSpec((128, 128), lambda i, place: (0, 0))],
            out_specs=[
                pl.BlockSpec((1, 8), lambda i, place: (0, 0)),
                pl.BlockSpec((1, 1), lambda i, place: (0, 0)),
            ],
        ),
        out_shape=[
            jax.ShapeDtypeStruct((1, 8), F32),
            jax.ShapeDtypeStruct((1, 1), F32),
        ],
    )(place, received)


def on_device(feats, inverses, counts, w_embed, w_qkv, w_out, w_mlp, w_orb):
    me = lax.axis_index("state")
    packed = jnp.concatenate(
        [
            w_qkv[0, 0],
            w_out[0, 0],
            w_mlp[0, 0],
            jnp.pad(w_orb[0], ((0, 0), (0, 128 - ELEC))),
            jnp.concatenate([w_embed[0, :, 128 * j : 128 * j + 128] for j in range(4)], axis=0),
        ],
        axis=1,
    )
    packed = lax.all_gather(packed, "walk", axis=0, tiled=True)
    flat = jnp.pad(inverses[0].reshape(8, ELEC, HALF), ((0, 1), (0, 0), (0, 0)))
    flat = flat.reshape(3, 3, ELEC, HALF)
    flat = jnp.concatenate(
        [flat[:, 0], flat[:, 1], flat[:, 2], jnp.zeros((3, ELEC, 8), F32)], axis=2
    )
    local = jnp.concatenate([feats[0], flat], axis=0)
    partner = lax.ppermute(local, "state", [(i, i ^ 4) for i in range(8)])

    def along(block):
        wide = jnp.broadcast_to(block[None], (4,) + block.shape)
        return lax.all_to_all(
            wide, "state", 0, 0, axis_index_groups=[[0, 1, 2, 3], [4, 5, 6, 7]]
        )

    group = along(local)
    other = along(partner)
    high = me // 4
    low = me % 4
    near = [high * 4 + (low + i) % 4 for i in range(4)]
    far = [(1 - high) * 4 + i for i in range(4)]
    place = jnp.stack(near + far).astype(jnp.int32)
    table, own = networks(place, counts, local, group, other, packed)
    received = lax.all_to_all(
        table.reshape(128, 1, 128), ("state", "walk"), 0, 0, tiled=True
    )
    margin, penalty = margins(place, received.reshape(128, 128))
    return own[:, 0:8], margin, penalty[0, 0]


def solution(mesh):
    in_specs = (
        P("state", "walk", None, None),
        P("state", "walk", None, None, None),
        P("state"),
        P("state", "walk", None),
        P("state", None, "walk", None),
        P("state", None, "walk", None),
        P("state", None, "walk", None),
        P("state", "walk", None),
    )
    out_specs = (P("state", "walk"), P("state", None), P())
    return jax.shard_map(
        on_device, mesh=mesh, in_specs=in_specs, out_specs=out_specs, check_vma=False
    )
```

```python
import math

import jax
import jax.numpy as jnp
from jax import lax
from jax.experimental import pallas as pl
from jax.experimental.pallas import tpu as pltpu
from jax.sharding import PartitionSpec as P

ELEC = 80
HALF = 40
BF = jnp.bfloat16
F32 = jnp.float32
OUT_AT, MLP_AT, ORB_AT, EMB_AT, PACKED = 1536, 2048, 2560, 2688, 2816
SAFE = 90.0


def dot(left, right):
    return jnp.dot(left, right, preferred_element_type=F32)


def dot_nt(left, right):
    return lax.dot_general(
        left, right, (((1,), (1,)), ((), ())), preferred_element_type=F32
    )


def split(values):
    high = values.astype(BF)
    return high, (values - high.astype(F32)).astype(BF)


def dot3(left, right, product):
    left_high, left_low = split(left)
    right_high, right_low = split(right)
    return (
        product(left_high, right_high)
        + product(left_low, right_high)
        + product(left_high, right_low)
    )


def weight_dot(values, ref, precise):
    if precise:
        high, low = split(values)
        return dot(high, ref[0]) + dot(low, ref[0]) + dot(high, ref[1])
    return dot(values.astype(BF), ref[0])


def prepare(packed, w_in, w_back, w_mlp, w_orb, copies):
    shards = packed.shape[0] // 32
    copies[0].wait()
    parts = []
    for j in range(4):
        rows = [packed[i * 32 + 8 * j : i * 32 + 8 * j + 8, EMB_AT:PACKED] for i in range(shards)]
        parts.append(jnp.concatenate(rows, axis=0))
    embed = jnp.concatenate(parts, axis=1)
    centred = embed - jnp.mean(embed, axis=1, keepdims=True)

    def put(at, values):
        high, low = split(values)
        columns = slice(at, at + values.shape[1])
        w_in[0, 0:128, columns] = high
        w_in[0, 128:256, columns] = high
        w_in[1, 0:128, columns] = low

    put(0, embed)
    copies[1].wait()
    query = dot3(centred, packed[:, 0:512], dot) * (math.log2(math.e) / 8.0)
    copies[2].wait()
    keys = dot3(centred, packed[:, 512:1024], dot)
    copies[3].wait()
    values = dot3(centred, packed[:, 1024:1536], dot)
    lane = lax.broadcasted_iota(jnp.int32, (128, 128), 1)
    copies[4].wait()
    for head in range(8):
        pair = slice(128 * (head // 2), 128 * (head // 2) + 128)
        keep = (lane < 64) if head % 2 == 0 else (lane >= 64)
        put(512 + 128 * head, dot3(jnp.where(keep, query[:, pair], 0.0), keys[:, pair], dot_nt))
        back = dot3(jnp.where(keep, values[:, pair], 0.0), packed[pair, OUT_AT:MLP_AT], dot)
        high, low = split(back)
        w_back[0, 128 * head : 128 * head + 128, :] = high
        w_back[1, 128 * head : 128 * head + 128, :] = low
    copies[5].wait()
    for ref, at, width in ((w_mlp, MLP_AT, 512), (w_orb, ORB_AT, 128)):
        high, low = split(packed[:, at : at + width])
        ref[0] = high
        ref[1] = low


def centre(values):
    centred = values - jnp.mean(values, axis=1, keepdims=True)
    spread = jnp.mean(centred * centred, axis=1, keepdims=True)
    return centred, lax.rsqrt(spread + 1e-05)


def walkers_block(feats, inverse, weights, precise, shift, out):
    w_in, w_back, w_mlp, w_orb = weights
    number = feats.shape[0] // ELEC
    feats_high, feats_low = split(feats)
    hidden = dot(jnp.concatenate([feats_high, feats_low], axis=1), w_in[0, :, 0:512])
    if precise:
        hidden = hidden + dot(feats_high, w_in[1, 0:128, 0:512])
    yield
    _, scale = centre(hidden)
    high, low = split(feats * scale)
    yield
    query = dot(jnp.concatenate([high, low], axis=1), w_in[0, :, 512:1536])
    if precise:
        query = query + dot(high, w_in[1, 0:128, 512:1536])
    yield
    empty = jnp.zeros((128 - ELEC, 128), BF)
    nothing = jnp.zeros((128, 128), BF)

    def padded(values, w):
        return jnp.concatenate([values[ELEC * w : ELEC * w + ELEC], empty], axis=0)

    def keys(values, w):
        if number == 1:
            return padded(values, w)
        above = jnp.concatenate([padded(values, w), nothing], axis=1)
        below = jnp.concatenate([nothing, padded(values, w + 1)], axis=1)
        return jnp.concatenate([above, below], axis=0)

    def by_head(w):
        rows = query[ELEC * w : ELEC * w + ELEC]
        return jnp.concatenate([rows[:, 128 * h : 128 * h + 128] for h in range(8)], axis=0)

    scores = []
    for w in range(0, number, 2):
        pair = range(w, min(w + 2, number))
        stacked = jnp.concatenate([by_head(u) for u in pair], axis=1)
        right = keys(high, w)
        if precise:
            stacked_high, stacked_low = split(stacked)
            score = (
                dot_nt(stacked_high, right)
                + dot_nt(stacked_low, right)
                + dot_nt(stacked_high, keys(low, w))
            )
        else:
            score = dot_nt(stacked.astype(BF), right)
        scores += [score[:, 128 * i : 128 * i + 128] for i in range(len(pair))]
    yield
    largest = jnp.zeros((8, 128), F32)
    lane = lax.broadcasted_iota(jnp.int32, (8 * ELEC, 128), 1)
    weights = []
    for score in scores:
        if shift:
            top = jnp.max(jnp.where(lane < ELEC, score, -jnp.inf), axis=1, keepdims=True)
            score = jnp.where(lane < ELEC, score - top, 0.0)
        else:
            sizes = jnp.abs(score).reshape(ELEC, 8, 128)
            largest = jnp.maximum(largest, jnp.max(sizes, axis=0))
        power = jnp.exp2(score)
        weights.append(split(power) if precise else power.astype(BF))
    yield
    row = lax.broadcasted_iota(jnp.int32, (128, 128), 0)
    live = jnp.where(row < ELEC, 1.0, 0.0).astype(BF)
    sums = []
    for w in range(number):
        right = jnp.concatenate([padded(high, w), live], axis=1)
        if precise:
            weights_high, weights_low = weights[w]
            both = dot(weights_high, right) + dot(weights_low, right)
            sums.append((both[:, :128] + dot(weights_high, padded(low, w)), both[:, 128:]))
        else:
            both = dot(weights[w], right)
            sums.append((both[:, :128], both[:, 128:]))
    yield
    mixed = []
    for top, bottom in sums:
        mean = top / bottom
        if not precise:
            mean = mean.astype(BF)
        mixed.append(
            jnp.concatenate([mean[ELEC * h : ELEC * h + ELEC] for h in range(8)], axis=1)
        )
    yield
    hidden = hidden + weight_dot(jnp.concatenate(mixed, axis=0), w_back, precise)
    yield
    centred, scale = centre(hidden)
    normal = centred * scale
    if not precise:
        normal = normal.astype(BF)
    yield
    inner = weight_dot(normal, w_mlp, precise)
    yield
    hidden = hidden + jnp.tanh(inner)
    if not precise:
        hidden = hidden.astype(BF)
    yield
    orbitals = weight_dot(hidden, w_orb, precise)
    yield
    lane = lax.broadcasted_iota(jnp.int32, (HALF, 128), 1)
    totals = []
    for first in range(0, number, 3):
        group = range(first, min(first + 3, number))
        rows = HALF * len(group)
        total = jnp.zeros((rows, 128), F32)
        lanes = lax.broadcasted_iota(jnp.int32, (rows, 128), 1)
        for spin in range(2):
            given = inverse(first // 3, spin)
            left = jnp.concatenate(
                [
                    jnp.where((lane >= HALF * i) & (lane < HALF * i + HALF), given, 0.0)
                    for i in range(len(group))
                ],
                axis=0,
            )
            at = HALF * spin
            right = jnp.concatenate(
                [orbitals[ELEC * w + at : ELEC * w + at + HALF] for w in group]
                + [jnp.zeros((128 - rows, 128), F32)],
                axis=0,
            )
            left_high, left_low = split(left)
            right_high, right_low = split(right)
            product = dot(
                jnp.concatenate([left_high, left_low], axis=1),
                jnp.concatenate([right_high, right_high], axis=0),
            ) + dot(left_high, right_low)
            product = jnp.where((lanes >= at) & (lanes < at + HALF), product, 0.0)
            total = total + product * product
        for i in range(len(group)):
            totals.append(jnp.sum(total[HALF * i : HALF * i + HALF], axis=0, keepdims=True))
    total = jnp.sum(jnp.concatenate(totals, axis=0), axis=1, keepdims=True)
    out.append((jnp.log(total / (2.0 * HALF * HALF) + 1e-05), largest))


def interleaved(blocks):
    waiting, running = list(blocks), []
    while waiting or running:
        if waiting:
            running.append(waiting.pop(0))
        running = [block for block in running if next(block, 0) is None]


def pack_kernel(feats, inverses, w_embed, w_qkv, w_out, w_mlp, w_orb, packed, local):
    packed[:, 0:OUT_AT] = w_qkv[0, 0]
    packed[:, OUT_AT:MLP_AT] = w_out[0, 0]
    packed[:, MLP_AT:ORB_AT] = w_mlp[0, 0]
    packed[:, ORB_AT:EMB_AT] = jnp.concatenate(
        [w_orb[0], jnp.zeros((w_orb.shape[1], 128 - ELEC), F32)], axis=1
    )
    for j in range(4):
        packed[8 * j : 8 * j + 8, EMB_AT:PACKED] = w_embed[0, :, 128 * j : 128 * j + 128]
    local[0:8] = feats[0]
    for group in range(3):
        for spin in range(2):
            parts = [
                inverses[0, w, spin] if w < 8 else jnp.zeros((HALF, HALF), F32)
                for w in range(3 * group, 3 * group + 3)
            ]
            parts.append(jnp.zeros((HALF, 8), F32))
            local[8 + group, HALF * spin : HALF * spin + HALF, :] = jnp.concatenate(parts, axis=1)


def pack(*arrays):
    return pl.pallas_call(
        pack_kernel,
        out_shape=[
            jax.ShapeDtypeStruct((32, PACKED), F32),
            jax.ShapeDtypeStruct((11, ELEC, 128), F32),
        ],
        compiler_params=pltpu.CompilerParams(vmem_limit_bytes=58 * 2**20),
    )(*arrays)


def evaluate(jobs, weights, rows):
    outs = [[] for _ in jobs]

    def inverse_of(pack):
        return lambda group, spin: pack[8 + group, HALF * spin : HALF * spin + HALF, :]

    interleaved(
        walkers_block(
            pack[0:8].reshape(8 * ELEC, 128), inverse_of(pack), weights, precise, False, out
        )
        for (pack, _, precise), out in zip(jobs, outs)
    )
    lane = lax.broadcasted_iota(jnp.int32, (8, 128), 1)
    walker = lax.broadcasted_iota(jnp.int32, (8, 128), 0)
    for i, (pack, first, precise) in enumerate(jobs):
        results, largest = outs[i][0]
        rows[i : i + 1] = jnp.sum(
            jnp.where(lane == first + walker, results, 0.0), axis=0, keepdims=True
        )

        @pl.when(jnp.logical_not(jnp.max(largest) < SAFE))
        def _(i=i, pack=pack, first=first, precise=precise):
            rows[i : i + 1] = jnp.zeros((1, 128), F32)

            @pl.loop(0, 8)
            def _(w):
                turn = lax.rem(128 - HALF * lax.rem(w, 3), 128)
                group = w // 3

                def inverse(_, spin):
                    part = pack[8 + group, HALF * spin : HALF * spin + HALF, :]
                    return pltpu.roll(part, turn, 1)

                out = []
                interleaved([walkers_block(pack[w], inverse, weights, precise, True, out)])
                rows[i : i + 1] += jnp.where(lane[0:1] == first + w, out[0][0], 0.0)


def near_kernel(
    place, counts, local, group, packed, table, own, w_in, w_back, w_mlp, w_orb,
    in_all, back_all, mlp_all, orb_all, wide, rows, sems
):
    step = pl.program_id(0)
    state = place[0]
    low = lax.rem(state, 4)
    lane = lax.broadcasted_iota(jnp.int32, (1, 128), 1)

    def near(i):
        at = lax.rem(low + i, 4)
        return group.at[at], (state - low + at) * 8, False

    @pl.when(step == 0)
    def _():
        edges = [(ORB_AT, PACKED)] + [(at, at + 512) for at in range(0, ORB_AT, 512)]
        copies = []
        for i, (start, stop) in enumerate(edges):
            copies.append(
                pltpu.make_async_copy(
                    packed.at[:, start:stop], wide.at[:, start:stop], sems.at[i]
                )
            )
            copies[-1].start()
        prepare(wide, in_all, back_all, mlp_all, orb_all, copies)
        w_in[0] = in_all[0]
        w_back[0] = back_all[0]
        w_mlp[0] = mlp_all[0]
        w_orb[0] = orb_all[0]
        evaluate(
            [(local, state * 8, True), near(1)], (in_all, back_all, mlp_all, orb_all), rows
        )
        first = rows[0:1]
        turned = jnp.zeros((1, 128), F32)
        for s in range(8):
            mine = (lane < 8) & (state == s)
            turned = turned + jnp.where(mine, pltpu.roll(first, (128 - 8 * s) % 128, 1), 0.0)
        own[...] = turned
        table[...] = (
            first + rows[1:2] + jnp.where(lane == 64, counts[0].astype(F32), 0.0)
        )

    @pl.when(step > 0)
    def _():
        evaluate([near(2), near(3)], (in_all, back_all, mlp_all, orb_all), rows)
        table[...] += rows[0:1] + rows[1:2]


def far_kernel(place, start, group, w_in, w_back, w_mlp, w_orb, table, rows):
    step = pl.program_id(0)
    first = lax.rem(place[0] // 4 + 1, 2) * 4

    @pl.when(step == 0)
    def _():
        table[...] = jnp.broadcast_to(start[...], table.shape)

    evaluate(
        [(group.at[2 * step + i], (first + 2 * step + i) * 8, False) for i in range(2)],
        (w_in, w_back, w_mlp, w_orb),
        rows,
    )
    table[...] += jnp.broadcast_to(rows[0:1] + rows[1:2], table.shape)


def hold(*zeros):
    return lambda i, *scalars: zeros


def networks(place, counts, local, group, other, packed):
    weights = [(256, 1536), (1024, 512), (512, 512), (512, 128)]
    whole = [pl.BlockSpec((1,) + shape, hold(0, 0, 0)) for shape in weights]
    params = pltpu.CompilerParams(vmem_limit_bytes=50 * 2**20)
    rows = pltpu.VMEM((8, 128), F32)
    start, own, *prepared = pl.pallas_call(
        near_kernel,
        grid_spec=pltpu.PrefetchScalarGridSpec(
            num_scalar_prefetch=2,
            grid=(2,),
            in_specs=[
                pl.BlockSpec((11, ELEC, 128), hold(0, 0, 0)),
                pl.BlockSpec((4, 11, ELEC, 128), hold(0, 0, 0, 0)),
                pl.BlockSpec(memory_space=pl.ANY),
            ],
            out_specs=[pl.BlockSpec((1, 128), hold(0, 0)), pl.BlockSpec((1, 128), hold(0, 0))]
            + whole,
            scratch_shapes=[pltpu.VMEM((2,) + shape, BF) for shape in weights]
            + [pltpu.VMEM((512, PACKED), F32), rows, pltpu.SemaphoreType.DMA((6,))],
        ),
        out_shape=[jax.ShapeDtypeStruct((1, 128), F32)] * 2
        + [jax.ShapeDtypeStruct((1,) + shape, BF) for shape in weights],
        compiler_params=params,
        cost_estimate=pl.CostEstimate(
            flops=20_000_000_000, bytes_accessed=10_000_000, transcendentals=5_000_000
        ),
    )(place, counts, local, group, packed)
    table = pl.pallas_call(
        far_kernel,
        grid_spec=pltpu.PrefetchScalarGridSpec(
            num_scalar_prefetch=1,
            grid=(2,),
            in_specs=[
                pl.BlockSpec((1, 128), hold(0, 0)),
                pl.BlockSpec((4, 11, ELEC, 128), hold(0, 0, 0, 0)),
            ]
            + whole,
            out_specs=pl.BlockSpec((128, 128), hold(0, 0)),
            scratch_shapes=[rows],
        ),
        out_shape=jax.ShapeDtypeStruct((128, 128), F32),
        compiler_params=params,
        cost_estimate=pl.CostEstimate(
            flops=15_000_000_000, bytes_accessed=10_000_000, transcendentals=5_000_000
        ),
    )(place, start, other, *prepared)
    return table, own


def margin_kernel(place, received, margin, penalty):
    table = received[...]
    lane = lax.broadcasted_iota(jnp.int32, (16, 128), 1)
    block = lax.broadcasted_iota(jnp.int32, (16, 128), 0)
    owner = lane // 8
    own = jnp.zeros((16, 128), F32)
    counts = jnp.ones((1, 128), F32)
    for s in range(8):
        own = jnp.where(owner == s, table[16 * s : 16 * s + 16], own)
        counts = jnp.where(owner[0:1] == s, table[16 * s : 16 * s + 1, 64:65], counts)
    walker = (block * 8 + lane % 8).astype(F32)
    valid = (walker < counts) & (lane < 64)
    rows = []
    for t in range(8):
        ratio = jnp.exp(jnp.where(valid, table[16 * t : 16 * t + 16] - own, -jnp.inf))
        rows.append(jnp.sum(ratio, axis=0, keepdims=True))
    sums = jnp.concatenate(rows, axis=0) / counts
    pick = (
        lax.broadcasted_iota(jnp.int32, (8, 128), 1) // 8
        == lax.broadcasted_iota(jnp.int32, (8, 128), 0)
    ).astype(F32)

    def exact(left, right):
        return lax.dot_general(
            left,
            right,
            (((1,), (1,)), ((), ())),
            precision=lax.Precision.HIGHEST,
            preferred_element_type=F32,
        )

    by_state = exact(pick, sums)
    by_network = exact(sums, pick)
    row = lax.broadcasted_iota(jnp.int32, (8, 8), 0)
    column = lax.broadcasted_iota(jnp.int32, (8, 8), 1)
    margin[...] = jnp.sum(jnp.where(row == place[0], by_state, 0.0), axis=0, keepdims=True)
    product = jnp.where(column < row, by_state * by_network, 0.0)
    total = jnp.sum(jnp.sum(product, axis=0, keepdims=True), axis=1, keepdims=True)
    penalty[...] = 4.0 * total


def margins(place, received):
    return pl.pallas_call(
        margin_kernel,
        grid_spec=pltpu.PrefetchScalarGridSpec(
            num_scalar_prefetch=1,
            grid=(1,),
            in_specs=[pl.BlockSpec((128, 128), lambda i, place: (0, 0))],
            out_specs=[
                pl.BlockSpec((1, 8), lambda i, place: (0, 0)),
                pl.BlockSpec((1, 1), lambda i, place: (0, 0)),
            ],
        ),
        out_shape=[
            jax.ShapeDtypeStruct((1, 8), F32),
            jax.ShapeDtypeStruct((1, 1), F32),
        ],
        compiler_params=pltpu.CompilerParams(vmem_limit_bytes=4 * 2**20),
    )(place, received)


def on_device(feats, inverses, counts, w_embed, w_qkv, w_out, w_mlp, w_orb):
    me = lax.axis_index("state")
    packed, local = pack(feats, inverses, w_embed, w_qkv, w_out, w_mlp, w_orb)
    packed = lax.all_gather(packed, "walk", axis=0, tiled=True)
    partner = lax.ppermute(local, "state", [(i, i ^ 4) for i in range(8)])

    def along(block):
        wide = jnp.broadcast_to(block[None], (4,) + block.shape)
        return lax.all_to_all(
            wide, "state", 0, 0, axis_index_groups=[[0, 1, 2, 3], [4, 5, 6, 7]]
        )

    group = along(local)
    other = along(partner)
    place = me[None].astype(jnp.int32)
    table, own = networks(place, counts, local, group, other, packed)
    received = lax.all_to_all(
        table.reshape(128, 1, 128), ("state", "walk"), 0, 0, tiled=True
    )
    margin, penalty = margins(place, received.reshape(128, 128))
    return own[:, 0:8], margin, penalty[0, 0]


def solution(mesh):
    in_specs = (
        P("state", "walk", None, None),
        P("state", "walk", None, None, None),
        P("state"),
        P("state", "walk", None),
        P("state", None, "walk", None),
        P("state", None, "walk", None),
        P("state", None, "walk", None),
        P("state", "walk", None),
    )
    out_specs = (P("state", "walk"), P("state", None), P())
    return jax.shard_map(
        on_device, mesh=mesh, in_specs=in_specs, out_specs=out_specs, check_vma=False
    )
```

```python
import math

import jax
import jax.numpy as jnp
from jax import lax
from jax.experimental import pallas as pl
from jax.experimental.pallas import tpu as pltpu
from jax.sharding import PartitionSpec as P

ELEC = 80
HALF = 40
BF = jnp.bfloat16
F32 = jnp.float32
OUT_AT, MLP_AT, ORB_AT, EMB_AT, PACKED = 1536, 2048, 2560, 2688, 2816
SAFE = 90.0


def dot(left, right):
    return jnp.dot(left, right, preferred_element_type=F32)


def dot_nt(left, right):
    return lax.dot_general(
        left, right, (((1,), (1,)), ((), ())), preferred_element_type=F32
    )


def split(values):
    high = values.astype(BF)
    return high, (values - high.astype(F32)).astype(BF)


def dot3(left, right, product):
    left_high, left_low = split(left)
    right_high, right_low = split(right)
    return (
        product(left_high, right_high)
        + product(left_low, right_high)
        + product(left_high, right_low)
    )


def weight_dot(values, ref, precise):
    if precise:
        high, low = split(values)
        return dot(high, ref[0]) + dot(low, ref[0]) + dot(high, ref[1])
    return dot(values.astype(BF), ref[0])


def prepare(packed, w_in, w_back, w_mlp, w_orb, copies):
    def fold(left, right):
        left_high, left_low = split(left)
        right_high, right_low = split(right)
        both = dot(jnp.concatenate([left_high, left_low], axis=0), right_high)
        return both[:128] + both[128:] + dot(left_high, right_low)

    copies[0].wait()
    parts = []
    for j in range(4):
        rows = [
            packed[i * 32 + 8 * j : i * 32 + 8 * j + 8, EMB_AT:PACKED] for i in range(16)
        ]
        parts.append(jnp.concatenate(rows, axis=0))
    embed = jnp.concatenate(parts, axis=1)
    centred = embed - jnp.mean(embed, axis=1, keepdims=True)

    def put(at, values):
        high, low = split(values)
        columns = slice(at, at + values.shape[1])
        w_in[0, 0:128, columns] = high
        w_in[0, 128:256, columns] = high
        w_in[1, 0:128, columns] = low

    put(0, embed)
    copies[1].wait()
    query = fold(centred, packed[:, 0:512]) * (math.log2(math.e) / 8.0)
    copies[2].wait()
    keys = fold(centred, packed[:, 512:1024])
    copies[3].wait()
    values = fold(centred, packed[:, 1024:1536])
    copies[4].wait()
    lane = lax.broadcasted_iota(jnp.int32, (128, 128), 1)

    def heads(matrix):
        return jnp.concatenate(
            [jnp.where(lane < 64, matrix, 0.0), jnp.where(lane >= 64, matrix, 0.0)], axis=0
        )

    for pair in range(4):
        at = slice(128 * pair, 128 * pair + 128)
        both = dot3(heads(query[:, at]), keys[:, at], dot_nt)
        put(512 + 256 * pair, both[:128])
        put(640 + 256 * pair, both[128:])
        both = dot3(heads(values[:, at]), packed[at, OUT_AT:MLP_AT], dot)
        high, low = split(both)
        w_back[0, 256 * pair : 256 * pair + 256, :] = high
        w_back[1, 256 * pair : 256 * pair + 256, :] = low
    copies[5].wait()
    for ref, at, width in ((w_mlp, MLP_AT, 512), (w_orb, ORB_AT, 128)):
        high, low = split(packed[:, at : at + width])
        ref[0] = high
        ref[1] = low


def centre(values):
    centred = values - jnp.mean(values, axis=1, keepdims=True)
    spread = jnp.mean(centred * centred, axis=1, keepdims=True)
    return centred, lax.rsqrt(spread + 1e-05)


def walkers_block(feats, inverse, weights, precise, shift, out):
    w_in, w_back, w_mlp, w_orb = weights
    number = feats.shape[0] // ELEC
    feats_high, feats_low = split(feats)
    hidden = dot(jnp.concatenate([feats_high, feats_low], axis=1), w_in[0, :, 0:512])
    if precise:
        hidden = hidden + dot(feats_high, w_in[1, 0:128, 0:512])
    yield
    _, scale = centre(hidden)
    high, low = split(feats * scale)
    yield
    query = dot(jnp.concatenate([high, low], axis=1), w_in[0, :, 512:1536])
    if precise:
        query = query + dot(high, w_in[1, 0:128, 512:1536])
    yield
    empty = jnp.zeros((128 - ELEC, 128), BF)
    nothing = jnp.zeros((128, 128), BF)

    def padded(values, w):
        return jnp.concatenate([values[ELEC * w : ELEC * w + ELEC], empty], axis=0)

    def keys(values, w):
        if number == 1:
            return padded(values, w)
        above = jnp.concatenate([padded(values, w), nothing], axis=1)
        below = jnp.concatenate([nothing, padded(values, w + 1)], axis=1)
        return jnp.concatenate([above, below], axis=0)

    def by_head(w):
        rows = query[ELEC * w : ELEC * w + ELEC]
        return jnp.concatenate([rows[:, 128 * h : 128 * h + 128] for h in range(8)], axis=0)

    scores = []
    for w in range(0, number, 2):
        pair = range(w, min(w + 2, number))
        stacked = jnp.concatenate([by_head(u) for u in pair], axis=1)
        right = keys(high, w)
        if precise:
            stacked_high, stacked_low = split(stacked)
            score = (
                dot_nt(stacked_high, right)
                + dot_nt(stacked_low, right)
                + dot_nt(stacked_high, keys(low, w))
            )
        else:
            score = dot_nt(stacked.astype(BF), right)
        scores += [score[:, 128 * i : 128 * i + 128] for i in range(len(pair))]
    yield
    largest = jnp.zeros((8, 128), F32)
    lane = lax.broadcasted_iota(jnp.int32, (8 * ELEC, 128), 1)
    weights = []
    for score in scores:
        if shift:
            top = jnp.max(jnp.where(lane < ELEC, score, -jnp.inf), axis=1, keepdims=True)
            score = jnp.where(lane < ELEC, score - top, 0.0)
        else:
            sizes = jnp.abs(score).reshape(ELEC, 8, 128)
            largest = jnp.maximum(largest, jnp.max(sizes, axis=0))
        power = jnp.exp2(score)
        weights.append(split(power) if precise else power.astype(BF))
    yield
    row = lax.broadcasted_iota(jnp.int32, (128, 128), 0)
    live = jnp.where(row < ELEC, 1.0, 0.0).astype(BF)
    sums = []
    for w in range(number):
        right = jnp.concatenate([padded(high, w), live], axis=1)
        if precise:
            weights_high, weights_low = weights[w]
            both = dot(
                jnp.concatenate([weights_high, weights_low], axis=1),
                jnp.concatenate([right, right], axis=0),
            )
            sums.append((both[:, :128] + dot(weights_high, padded(low, w)), both[:, 128:]))
        else:
            both = dot(weights[w], right)
            sums.append((both[:, :128], both[:, 128:]))
    yield
    mixed = []
    for top, bottom in sums:
        mean = top / bottom
        if not precise:
            mean = mean.astype(BF)
        mixed.append(
            jnp.concatenate([mean[ELEC * h : ELEC * h + ELEC] for h in range(8)], axis=1)
        )
    yield
    hidden = hidden + weight_dot(jnp.concatenate(mixed, axis=0), w_back, precise)
    yield
    centred, scale = centre(hidden)
    normal = centred * scale
    if not precise:
        normal = normal.astype(BF)
    yield
    inner = weight_dot(normal, w_mlp, precise)
    yield
    hidden = hidden + jnp.tanh(inner)
    if not precise:
        hidden = hidden.astype(BF)
    yield
    orbitals = weight_dot(hidden, w_orb, precise)
    yield
    lane = lax.broadcasted_iota(jnp.int32, (HALF, 128), 1)
    totals = []
    for first in range(0, number, 3):
        group = range(first, min(first + 3, number))
        rows = HALF * len(group)
        total = jnp.zeros((rows, 128), F32)
        lanes = lax.broadcasted_iota(jnp.int32, (rows, 128), 1)
        for spin in range(2):
            given = inverse(first // 3, spin)
            left = jnp.concatenate(
                [
                    jnp.where((lane >= HALF * i) & (lane < HALF * i + HALF), given, 0.0)
                    for i in range(len(group))
                ],
                axis=0,
            )
            at = HALF * spin
            right = jnp.concatenate(
                [orbitals[ELEC * w + at : ELEC * w + at + HALF] for w in group]
                + [jnp.zeros((128 - rows, 128), F32)],
                axis=0,
            )
            left_high, left_low = split(left)
            right_high, right_low = split(right)
            product = dot(
                jnp.concatenate([left_high, left_low], axis=1),
                jnp.concatenate([right_high, right_high], axis=0),
            ) + dot(left_high, right_low)
            product = jnp.where((lanes >= at) & (lanes < at + HALF), product, 0.0)
            total = total + product * product
        for i in range(len(group)):
            totals.append(jnp.sum(total[HALF * i : HALF * i + HALF], axis=0, keepdims=True))
    total = jnp.sum(jnp.concatenate(totals, axis=0), axis=1, keepdims=True)
    out.append((jnp.log(total / (2.0 * HALF * HALF) + 1e-05), largest))


def interleaved(blocks):
    waiting, running = list(blocks), []
    while waiting or running:
        if waiting:
            running.append(waiting.pop(0))
        running = [block for block in running if next(block, 0) is None]


def pack_weights_kernel(w_embed, w_qkv, w_out, w_mlp, w_orb, packed):
    packed[:, 0:OUT_AT] = w_qkv[0, 0]
    packed[:, OUT_AT:MLP_AT] = w_out[0, 0]
    packed[:, MLP_AT:ORB_AT] = w_mlp[0, 0]
    packed[:, ORB_AT:EMB_AT] = jnp.concatenate(
        [w_orb[0], jnp.zeros((w_orb.shape[1], 128 - ELEC), F32)], axis=1
    )
    for j in range(4):
        packed[8 * j : 8 * j + 8, EMB_AT:PACKED] = w_embed[0, :, 128 * j : 128 * j + 128]


def pack_walkers_kernel(feats, inverses, local, wide):
    local[0:8] = feats[0]
    for group in range(3):
        for spin in range(2):
            parts = [
                inverses[0, w, spin] if w < 8 else jnp.zeros((HALF, HALF), F32)
                for w in range(3 * group, 3 * group + 3)
            ]
            parts.append(jnp.zeros((HALF, 8), F32))
            local[8 + group, HALF * spin : HALF * spin + HALF, :] = jnp.concatenate(parts, axis=1)
    for to in range(4):
        wide[to] = local[...]


def pack(kernel, shapes, *arrays):
    return pl.pallas_call(
        kernel,
        out_shape=[jax.ShapeDtypeStruct(shape, F32) for shape in shapes],
        compiler_params=pltpu.CompilerParams(vmem_limit_bytes=58 * 2**20),
    )(*arrays)


def evaluate(jobs, weights, rows):
    outs = [[] for _ in jobs]

    def inverse_of(pack):
        return lambda group, spin: pack[8 + group, HALF * spin : HALF * spin + HALF, :]

    interleaved(
        walkers_block(
            pack[0:8].reshape(8 * ELEC, 128), inverse_of(pack), weights, precise, False, out
        )
        for (pack, _, precise), out in zip(jobs, outs)
    )
    lane = lax.broadcasted_iota(jnp.int32, (8, 128), 1)
    walker = lax.broadcasted_iota(jnp.int32, (8, 128), 0)
    for i, (pack, first, precise) in enumerate(jobs):
        results, largest = outs[i][0]
        rows[i : i + 1] = jnp.sum(
            jnp.where(lane == first + walker, results, 0.0), axis=0, keepdims=True
        )

        @pl.when(jnp.logical_not(jnp.max(largest) < SAFE))
        def _(i=i, pack=pack, first=first, precise=precise):
            rows[i : i + 1] = jnp.zeros((1, 128), F32)

            @pl.loop(0, 8)
            def _(w):
                turn = lax.rem(128 - HALF * lax.rem(w, 3), 128)
                group = w // 3

                def inverse(_, spin):
                    part = pack[8 + group, HALF * spin : HALF * spin + HALF, :]
                    return pltpu.roll(part, turn, 1)

                out = []
                interleaved([walkers_block(pack[w], inverse, weights, precise, True, out)])
                rows[i : i + 1] += jnp.where(lane[0:1] == first + w, out[0][0], 0.0)


def near_kernel(
    place, counts, local, group, packed, table, own, w_in, w_back, w_mlp, w_orb,
    in_all, back_all, mlp_all, orb_all, wide, rows, sems
):
    step = pl.program_id(0)
    state = place[0]
    low = lax.rem(state, 4)
    lane = lax.broadcasted_iota(jnp.int32, (1, 128), 1)

    def near(i):
        at = lax.rem(low + i, 4)
        return group.at[at], (state - low + at) * 8, False

    @pl.when(step == 0)
    def _():
        edges = [(ORB_AT, PACKED)] + [(at, at + 512) for at in range(0, ORB_AT, 512)]
        copies = []
        for i, (start, stop) in enumerate(edges):
            copies.append(
                pltpu.make_async_copy(
                    packed.at[:, start:stop], wide.at[:, start:stop], sems.at[i]
                )
            )
            copies[-1].start()
        prepare(wide, in_all, back_all, mlp_all, orb_all, copies)
        w_in[0] = in_all[0]
        w_back[0] = back_all[0]
        w_mlp[0] = mlp_all[0]
        w_orb[0] = orb_all[0]
        evaluate(
            [(local, state * 8, True), near(1)], (in_all, back_all, mlp_all, orb_all), rows
        )
        first = rows[0:1]
        turned = jnp.zeros((1, 128), F32)
        for s in range(8):
            mine = (lane < 8) & (state == s)
            turned = turned + jnp.where(mine, pltpu.roll(first, (128 - 8 * s) % 128, 1), 0.0)
        own[...] = turned
        table[...] = (
            first + rows[1:2] + jnp.where(lane == 64, counts[0].astype(F32), 0.0)
        )

    @pl.when(step > 0)
    def _():
        evaluate([near(2), near(3)], (in_all, back_all, mlp_all, orb_all), rows)
        table[...] += rows[0:1] + rows[1:2]


def far_kernel(place, start, group, w_in, w_back, w_mlp, w_orb, table, rows):
    step = pl.program_id(0)
    first = lax.rem(place[0] // 4 + 1, 2) * 4

    @pl.when(step == 0)
    def _():
        table[...] = jnp.broadcast_to(start[...], table.shape)

    evaluate(
        [(group.at[2 * step + i], (first + 2 * step + i) * 8, False) for i in range(2)],
        (w_in, w_back, w_mlp, w_orb),
        rows,
    )
    table[...] += jnp.broadcast_to(rows[0:1] + rows[1:2], table.shape)


def hold(*zeros):
    return lambda i, *scalars: zeros


def networks(place, counts, local, group, other, packed):
    weights = [(256, 1536), (1024, 512), (512, 512), (512, 128)]
    whole = [pl.BlockSpec((1,) + shape, hold(0, 0, 0)) for shape in weights]
    params = pltpu.CompilerParams(vmem_limit_bytes=50 * 2**20)
    rows = pltpu.VMEM((8, 128), F32)
    start, own, *prepared = pl.pallas_call(
        near_kernel,
        grid_spec=pltpu.PrefetchScalarGridSpec(
            num_scalar_prefetch=2,
            grid=(2,),
            in_specs=[
                pl.BlockSpec((11, ELEC, 128), hold(0, 0, 0)),
                pl.BlockSpec((4, 11, ELEC, 128), hold(0, 0, 0, 0)),
                pl.BlockSpec(memory_space=pl.ANY),
            ],
            out_specs=[pl.BlockSpec((1, 128), hold(0, 0)), pl.BlockSpec((1, 128), hold(0, 0))]
            + whole,
            scratch_shapes=[pltpu.VMEM((2,) + shape, BF) for shape in weights]
            + [pltpu.VMEM((512, PACKED), F32), rows, pltpu.SemaphoreType.DMA((6,))],
        ),
        out_shape=[jax.ShapeDtypeStruct((1, 128), F32)] * 2
        + [jax.ShapeDtypeStruct((1,) + shape, BF) for shape in weights],
        compiler_params=params,
        cost_estimate=pl.CostEstimate(
            flops=20_000_000_000, bytes_accessed=10_000_000, transcendentals=5_000_000
        ),
    )(place, counts, local, group, packed)
    table = pl.pallas_call(
        far_kernel,
        grid_spec=pltpu.PrefetchScalarGridSpec(
            num_scalar_prefetch=1,
            grid=(2,),
            in_specs=[
                pl.BlockSpec((1, 128), hold(0, 0)),
                pl.BlockSpec((4, 11, ELEC, 128), hold(0, 0, 0, 0)),
            ]
            + whole,
            out_specs=pl.BlockSpec((128, 128), hold(0, 0)),
            scratch_shapes=[rows],
        ),
        out_shape=jax.ShapeDtypeStruct((128, 128), F32),
        compiler_params=params,
        cost_estimate=pl.CostEstimate(
            flops=15_000_000_000, bytes_accessed=10_000_000, transcendentals=5_000_000
        ),
    )(place, start, other, *prepared)
    return table, own


def margin_kernel(place, received, margin, penalty):
    table = received[...]
    lane = lax.broadcasted_iota(jnp.int32, (16, 128), 1)
    block = lax.broadcasted_iota(jnp.int32, (16, 128), 0)
    owner = lane // 8
    own = jnp.zeros((16, 128), F32)
    counts = jnp.ones((1, 128), F32)
    for s in range(8):
        own = jnp.where(owner == s, table[16 * s : 16 * s + 16], own)
        counts = jnp.where(owner[0:1] == s, table[16 * s : 16 * s + 1, 64:65], counts)
    walker = (block * 8 + lane % 8).astype(F32)
    valid = (walker < counts) & (lane < 64)
    rows = []
    for t in range(8):
        ratio = jnp.exp(jnp.where(valid, table[16 * t : 16 * t + 16] - own, -jnp.inf))
        rows.append(jnp.sum(ratio, axis=0, keepdims=True))
    sums = jnp.concatenate(rows, axis=0) / counts
    pick = (
        lax.broadcasted_iota(jnp.int32, (8, 128), 1) // 8
        == lax.broadcasted_iota(jnp.int32, (8, 128), 0)
    ).astype(F32)

    def exact(left, right):
        return lax.dot_general(
            left,
            right,
            (((1,), (1,)), ((), ())),
            precision=lax.Precision.HIGHEST,
            preferred_element_type=F32,
        )

    by_state = exact(pick, sums)
    by_network = exact(sums, pick)
    row = lax.broadcasted_iota(jnp.int32, (8, 8), 0)
    column = lax.broadcasted_iota(jnp.int32, (8, 8), 1)
    margin[...] = jnp.sum(jnp.where(row == place[0], by_state, 0.0), axis=0, keepdims=True)
    product = jnp.where(column < row, by_state * by_network, 0.0)
    total = jnp.sum(jnp.sum(product, axis=0, keepdims=True), axis=1, keepdims=True)
    penalty[...] = 4.0 * total


def margins(place, received):
    return pl.pallas_call(
        margin_kernel,
        grid_spec=pltpu.PrefetchScalarGridSpec(
            num_scalar_prefetch=1,
            grid=(1,),
            in_specs=[pl.BlockSpec((128, 128), lambda i, place: (0, 0))],
            out_specs=[
                pl.BlockSpec((1, 8), lambda i, place: (0, 0)),
                pl.BlockSpec((1, 1), lambda i, place: (0, 0)),
            ],
        ),
        out_shape=[
            jax.ShapeDtypeStruct((1, 8), F32),
            jax.ShapeDtypeStruct((1, 1), F32),
        ],
        compiler_params=pltpu.CompilerParams(vmem_limit_bytes=4 * 2**20),
    )(place, received)


def on_device(feats, inverses, counts, w_embed, w_qkv, w_out, w_mlp, w_orb):
    me = lax.axis_index("state")
    (packed,) = pack(
        pack_weights_kernel, [(32, PACKED)], w_embed, w_qkv, w_out, w_mlp, w_orb
    )
    packed = lax.all_gather(packed, "walk", axis=0, tiled=True)
    local, wide = pack(
        pack_walkers_kernel, [(11, ELEC, 128), (4, 11, ELEC, 128)], feats, inverses
    )
    along = [[0, 1, 2, 3], [4, 5, 6, 7]]
    group = lax.all_to_all(wide, "state", 0, 0, axis_index_groups=along)
    partner = lax.ppermute(local, "state", [(i, i ^ 4) for i in range(8)])
    wide = jnp.broadcast_to(partner[None], (4,) + partner.shape)
    other = lax.all_to_all(wide, "state", 0, 0, axis_index_groups=along)
    place = me[None].astype(jnp.int32)
    table, own = networks(place, counts, local, group, other, packed)
    received = lax.all_to_all(
        table.reshape(128, 1, 128), ("state", "walk"), 0, 0, tiled=True
    )
    margin, penalty = margins(place, received.reshape(128, 128))
    return own[:, 0:8], margin, penalty[0, 0]


def solution(mesh):
    in_specs = (
        P("state", "walk", None, None),
        P("state", "walk", None, None, None),
        P("state"),
        P("state", "walk", None),
        P("state", None, "walk", None),
        P("state", None, "walk", None),
        P("state", None, "walk", None),
        P("state", "walk", None),
    )
    out_specs = (P("state", "walk"), P("state", None), P())
    return jax.shard_map(
        on_device, mesh=mesh, in_specs=in_specs, out_specs=out_specs, check_vma=False
    )
```
